256 devices in a mesh: row: 8 (over x, y_lo), col: 32 (over z, y_hi, core).
Axes of the slice: x: 4, y: 4 (y_hi: 2, y_lo: 2; y = y_hi * 2 + y_lo), z: 8, core: 2. Of those that a mesh axis runs over, the one named last changes fastest.
Arguments:
- node_feat: bfloat16 [262144, 128], P(('row', 'col')), may hold values from -6 to 6
- tile_cols: int32 [2048, 40], P(('row', 'col')), may hold values from 0 to 255, as said below
- tile_vals: bfloat16 [2048, 40, 128, 128], P(('row', 'col')), may hold values from 0 to 1, as said below
- tile_count: int32 [2048], P(('row', 'col')), may hold values from 1 to 40, as said below
- w_self: bfloat16 [128, 256], replicated, may hold values from -0.5 to 0.5
- w_neigh: bfloat16 [128, 256], replicated, may hold values from -0.5 to 0.5
- layer_bias: float32 [256], replicated, may hold values from -3 to 3
- grad_out: bfloat16 [262144, 256], P(('row', 'col')), may hold values from -6 to 6
Outputs:
- activation: bfloat16 [262144, 256], P(('row', 'col'))
- grad_feat: bfloat16 [262144, 128], P(('row', 'col'))
- grad_w_self: float32 [128, 256], replicated
- grad_w_neigh: float32 [128, 256], replicated
- grad_bias: float32 [256], replicated
The draws below stay inside these ranges and needn't reach their ends.
Inputs may be any that keep to these rules, and one draw needn't show every extreme that they name: Tile row t covers nodes t*128 to t*128 + 127 and lies in grid row r = t // 256; entry [t, k] names the column tile of nodes r*32768 + tile_cols[t, k]*128 onward. The live slots of a row (k < tile_count[t]) name distinct tiles, slot 0 the row's own diagonal tile t % 256; slots past the count name the diagonal tile as well. The pattern is symmetric: if live slot k of tile row t in grid row r names tile b, then tile row r*256 + b has a live slot naming t % 256, whose block is the transpose of tile_vals[t, k]. A diagonal block is symmetric with ones on its diagonal; blocks of slots past the count are zero. `tile_count`: the number of live slots of each tile row; in every grid row some tile row has 40 and some has 1.
All inputs are finite; a program needn't handle non-finite values.
Results may differ from the reference program's by a relative error of at most 0.0045.
Values may be sent and summed in bfloat16 or wider, within the bound.
No kernel may reach another device: no remote copies, remote signals or barrier semaphores. Data moves between devices by JAX's collectives and lax.ppermute only.
A program may use at most 128 MiB of HBM per device.

```python
import math
import jax
import jax.numpy as jnp
from jax import lax

F = 128
HID = 256
TS = 128
KPR = 40
NODES = 262144
ROWS_TILE = 8
SLAB_TILES = 256
TILE_ROWS = 2048
N_ROW = 8
N_COL = 32


def tile_layout(key):

    def one_slab(slab_key):
        sub_keys = jax.random.split(slab_key, 5)
        extent = SLAB_TILES
        anchor = jax.random.randint(sub_keys[0], (), 0, extent)
        excluded = 2 * anchor % extent
        shuffled = jax.random.permutation(sub_keys[1], extent)
        reordered = shuffled[jnp.argsort((shuffled == excluded).astype(jnp.int32), stable=True)]
        offsets = reordered[:KPR - 1]
        empty_row = (reordered[KPR - 1] - anchor) % extent
        placing = jax.random.permutation(sub_keys[2], extent)
        levels = jnp.array([1, 2, 4, 8], jnp.int32)[jax.random.randint(sub_keys[3], (N_COL,), 0, 4)]
        tickets = jax.random.randint(sub_keys[4], (extent, KPR - 1), 0, 64)
        logical = jnp.arange(extent)[:, None]
        partner = (offsets[None, :] - logical) % extent
        lower_index = jnp.minimum(logical, partner)
        ticket = tickets[lower_index, jnp.arange(KPR - 1)[None, :]]
        demand = levels[placing[logical] // ROWS_TILE] * levels[placing[partner] // ROWS_TILE]
        present = (ticket < demand) | (logical == anchor) | (partner == anchor)
        present = present & (logical != empty_row) & (partner != empty_row) & (partner != logical)
        every_live = jnp.concatenate([jnp.ones((extent, 1), jnp.bool_), present], axis=1)
        every_partner = jnp.concatenate([logical, partner], axis=1)
        slot_index = jnp.arange(KPR)[None, :]
        slot_order = jnp.argsort(jnp.where(every_live, slot_index, KPR + slot_index), axis=1, stable=True)
        live_sorted = jnp.take_along_axis(every_live, slot_order, axis=1)
        partner_sorted = jnp.take_along_axis(every_partner, slot_order, axis=1)
        column = jnp.where(live_sorted, placing[partner_sorted], placing[logical])
        live_count = jnp.sum(live_sorted.astype(jnp.int32), axis=1)
        by_place = jnp.argsort(placing)
        return (column[by_place], live_count[by_place], live_sorted[by_place], partner_sorted[by_place], slot_order[by_place], by_place)
    return jax.vmap(one_slab)(jax.random.split(key, N_ROW))


def draw_tile_cols(key, part):
    layout = tile_layout(key)
    return layout[0].reshape(TILE_ROWS, KPR).astype(jnp.int32)


def draw_tile_count(key, part):
    layout = tile_layout(key)
    return layout[1].reshape(TILE_ROWS).astype(jnp.int32)


def draw_tile_vals(key, part):
    layout = tile_layout(key)
    key = jax.random.fold_in(key, 7)
    rows_index = jnp.arange(TS)[:, None]
    cols_index = jnp.arange(TS)[None, :]

    def make_tile(tile_key, own_index, partner_node, slot_index, slot_alive):
        pair_key = jax.random.fold_in(tile_key, jnp.minimum(own_index, partner_node) * KPR + slot_index)
        mask_key, value_key = jax.random.split(pair_key)
        present_entry = (jax.random.randint(mask_key, (TS, TS), 0, 4) == 0).astype(jnp.float32)
        strength = jnp.exp(jax.random.uniform(value_key, (TS, TS), jnp.float32, math.log(0.1), 0.0))
        raw_tile = present_entry * strength
        flipped = raw_tile.T
        mirrored = jnp.where(rows_index < cols_index, raw_tile, flipped)
        mirrored = jnp.where(rows_index == cols_index, 1.0, mirrored)
        chosen = jnp.where(slot_index == 0, mirrored, jnp.where(own_index > partner_node, flipped, raw_tile))
        return jnp.where(slot_alive, chosen, 0.0)

    def one_slab(inputs):
        slab_key, live_rows, partner_rows, slot_rows, own_rows = inputs

        def one_row(row_data):
            live_row, partner_row, slot_row, own_index = row_data

            def one_slot(partner_node, slot_index, slot_alive):
                return make_tile(slab_key, own_index, partner_node, slot_index, slot_alive)
            tile_block = jax.vmap(one_slot)(partner_row, slot_row, live_row)
            return tile_block.astype(jnp.bfloat16)
        return lax.map(one_row, (live_rows, partner_rows, slot_rows, own_rows))
    slab_keys = jax.random.split(key, N_ROW)
    tile_block = lax.map(one_slab, (slab_keys, layout[2], layout[3], layout[4], layout[5]))
    return tile_block.reshape(TILE_ROWS, KPR, TS, TS)


def block_scale(stream_key, dims, cuts, smallest, largest):
    loudness, own = 1.0, jax.random.fold_in(stream_key, 6)
    for axis_at, parts in cuts:
        steps = jnp.exp(jax.random.uniform(jax.random.fold_in(own, axis_at), (parts,), jnp.float32, smallest / len(cuts), largest / len(cuts)))
        loudness = loudness * jnp.repeat(steps, dims[axis_at] // parts).reshape([-1 if axis == axis_at else 1 for axis in range(len(dims))])
    return loudness


def bell_draw(own_key, dims, width, limit, cuts=(), kind=jnp.bfloat16):
    drawn = width * jax.random.normal(own_key, dims, jnp.float32)
    if cuts:
        drawn = drawn * block_scale(own_key, dims, cuts, -0.22, 0.18)
    return jnp.clip(drawn, -limit, limit).astype(kind)


def setup_inputs(seed: int = 0) -> dict:
    seeds = jax.random.split(jax.random.key(seed), 9)
    return {
        "node_feat": bell_draw(seeds[0], (NODES, F), 1.0, 6.0, ((0, 256),)),
        "tile_cols": draw_tile_cols(jax.random.fold_in(seeds[8], 71), 0),
        "tile_vals": draw_tile_vals(jax.random.fold_in(seeds[8], 71), 0),
        "tile_count": draw_tile_count(jax.random.fold_in(seeds[8], 71), 0),
        "w_self": bell_draw(seeds[4], (F, HID), F ** -0.5, 0.5),
        "w_neigh": bell_draw(seeds[5], (F, HID), F ** -0.5, 0.5),
        "layer_bias": bell_draw(seeds[6], (HID,), 0.5, 3.0, (), jnp.float32),
        "grad_out": bell_draw(seeds[7], (NODES, HID), 1.0, 6.0, ((0, 256),)),
    }


def reference(node_feat, tile_cols, tile_vals, tile_count, w_self, w_neigh, layer_bias, grad_out):
    slot_live = (jnp.arange(KPR)[None, :] < tile_count[:, None]).astype(jnp.float32)
    row_sums = lax.optimization_barrier(jnp.sum(tile_vals, axis=3, dtype=jnp.float32))
    degree = lax.optimization_barrier(jnp.sum(row_sums * slot_live[:, :, None], axis=1)).reshape(NODES)
    inv_root = lax.rsqrt(degree)[:, None]
    slab_cols = tile_cols.reshape(N_ROW, SLAB_TILES, KPR)
    slab_vals = tile_vals.reshape(N_ROW, SLAB_TILES, KPR, TS, TS)
    slab_live = slot_live.reshape(N_ROW, SLAB_TILES, KPR)

    def forward_slab(inputs):
        source, col_rows, val_rows, live_rows = inputs

        def one_row(row_data):
            col_row, val_row, live_row = row_data
            picked = source[col_row].astype(jnp.float32) * live_row[:, None, None]
            return jnp.einsum('kab,kbf->af', val_row.astype(jnp.float32), picked, precision=lax.Precision.HIGHEST)
        return lax.map(one_row, (col_rows, val_rows, live_rows))
    sources = node_feat.reshape(N_ROW, SLAB_TILES, TS, F)
    neighbour_sum = lax.map(forward_slab, (sources, slab_cols, slab_vals, slab_live)).reshape(NODES, F)
    aggregated = (neighbour_sum * inv_root).astype(jnp.bfloat16)
    preact = jnp.dot(node_feat, w_self, preferred_element_type=jnp.float32) + jnp.dot(aggregated, w_neigh, preferred_element_type=jnp.float32) + layer_bias
    positive = preact > 0.0
    activation = jnp.where(positive, preact, jnp.expm1(preact)).astype(jnp.bfloat16)
    derivative = jnp.where(positive, jnp.float32(1.0), jnp.exp(preact))
    grad_preact = (grad_out.astype(jnp.float32) * derivative).astype(jnp.bfloat16)
    grad_scale = 1.0 / math.sqrt(NODES)
    grad_w_self = jnp.dot(node_feat.T, grad_preact, preferred_element_type=jnp.float32) * grad_scale
    grad_w_neigh = jnp.dot(aggregated.T, grad_preact, preferred_element_type=jnp.float32) * grad_scale
    grad_bias = lax.optimization_barrier(jnp.sum(grad_preact.astype(jnp.float32), axis=0)) * grad_scale
    scaled_back = (jnp.dot(grad_preact, w_neigh.T, preferred_element_type=jnp.float32) * inv_root).astype(jnp.bfloat16)

    def backward_slab(inputs):
        source, col_rows, val_rows, live_rows = inputs

        def add_row(summed, row_data):
            col_row, val_row, live_row, back_row = row_data
            pieces = jnp.einsum('kab,af->kbf', val_row.astype(jnp.float32), back_row.astype(jnp.float32), precision=lax.Precision.HIGHEST) * live_row[:, None, None]
            return (summed.at[col_row].add(pieces), None)
        summed, unused = lax.scan(add_row, jnp.zeros((SLAB_TILES, TS, F), jnp.float32), (col_rows, val_rows, live_rows, source))
        return summed
    back_sources = scaled_back.reshape(N_ROW, SLAB_TILES, TS, F)
    neigh_back = lax.map(backward_slab, (back_sources, slab_cols, slab_vals, slab_live)).reshape(NODES, F)
    grad_feat = (jnp.dot(grad_preact, w_self.T, preferred_element_type=jnp.float32) + neigh_back).astype(jnp.bfloat16)
    return (activation, grad_feat, grad_w_self, grad_w_neigh, grad_bias)
```

```python
import math

import jax
import jax.numpy as jnp
from jax import lax
from jax.experimental import pallas as pl
from jax.experimental.pallas import tpu as pltpu
from jax.sharding import PartitionSpec as P

SIDE = 128
GROUP = 8


def col_index(z, y, k):
    return (z % 8) * 4 + (y % 2) * 2 + (k % 2)


def col_perm(dz, dy, dk):
    return [
        (col_index(z, y, k), col_index(z + dz, y + dy, k + dk))
        for z in range(8)
        for y in range(2)
        for k in range(2)
    ]


def move(x, dz, dy, dk):
    return lax.ppermute(x, "col", col_perm(dz, dy, dk))


def gather_slab(x):
    n = x.shape[0]
    half = n // 2
    swapped = move(x, 0, 1, 0)
    pair = jnp.concatenate([x, swapped], axis=0)
    pieces = [(pair, [(0, n, 0, 0, 0, 0), (n, n, 0, 1, 0, 0)])]
    up = down = pair
    for step in range(1, 4):
        up, down = move(up, 1, 0, 0), move(down, -1, 0, 0)
        pieces.append((up, [(0, n, -step, 0, 0, 0), (n, n, -step, 1, 0, 0)]))
        pieces.append((down, [(0, n, step, 0, 0, 0), (n, n, step, 1, 0, 0)]))
    up, down = move(up[:n], 1, 0, 0), move(down[n:], -1, 0, 0)
    pieces.append((up, [(0, n, 4, 0, 0, 0)]))
    pieces.append((down, [(0, n, 4, 1, 0, 0)]))
    crossed = [
        (move(a, 0, 0, 1), [(r, m, dz, dy, 1, b) for r, m, dz, dy, _, b in where])
        for a, where in pieces
    ]
    return pieces + crossed


def fill_slab(place_ref, piece_refs, wheres, slab, sems, block_rows):
    z, y, k = place_ref[0], place_ref[1], place_ref[2]
    copies = []
    for ref, where in zip(piece_refs, wheres):
        for r, m, dz, dy, dk, b in where:
            home = lax.rem(z + (dz + 8), 8) * 4 + lax.rem(y + dy, 2) * 2 + lax.rem(k + dk, 2)
            start = pl.multiple_of(home * block_rows + b, SIDE)
            copies.append(
                pltpu.make_async_copy(
                    ref.at[pl.ds(r, m)], slab.at[pl.ds(start, m)], sems.at[len(copies)]
                )
            )
    for c in copies:
        c.start()
    for c in copies:
        c.wait()


def row_product(t, cols_ref, count_ref, vals_ref, slab, with_ones):
    width = 2 * SIDE if with_ones else SIDE

    def body(i, acc):
        left, right = [], []
        for j in range(GROUP):
            slot = i * GROUP + j
            left.append(vals_ref[0, slot])
            start = pl.multiple_of(cols_ref[t, slot] * SIDE, SIDE)
            right.append(slab[pl.ds(start, SIDE), :])
        rhs = jnp.concatenate(right, axis=0)
        if with_ones:
            rhs = jnp.concatenate([rhs, jnp.ones_like(rhs)], axis=1)
        lhs = jnp.concatenate(left, axis=1)
        return acc + jnp.dot(lhs, rhs, preferred_element_type=jnp.float32)

    trips = (count_ref[t] + (GROUP - 1)) // GROUP
    return lax.fori_loop(0, trips, body, jnp.zeros((SIDE, width), jnp.float32))


def forward_kernel(wheres, block_rows):
    count = len(wheres)

    def kernel(cols_ref, count_ref, place_ref, vals_ref, x_ref, g_ref, w_ref, wt_ref, bias_ref, *rest):
        piece_refs = rest[:count]
        act_ref, back_ref, self_ref, both_ref, gp_ref, slab, sems = rest[count:]
        t = pl.program_id(0)

        @pl.when(t == 0)
        def _():
            fill_slab(place_ref, piece_refs, wheres, slab, sems, block_rows)

        acc = row_product(t, cols_ref, count_ref, vals_ref, slab, True)
        inv_root = lax.rsqrt(acc[:, SIDE:])
        aggregated = (acc[:, :SIDE] * inv_root).astype(jnp.bfloat16)
        both = jnp.concatenate([x_ref[...], aggregated], axis=1)
        both_ref[...] = both
        preact = jnp.dot(both, w_ref[...], preferred_element_type=jnp.float32) + bias_ref[...]
        positive = preact > 0.0
        grown = jnp.exp(jnp.minimum(preact, 0.0))
        act_ref[...] = jnp.where(positive, preact, grown - 1.0).astype(jnp.bfloat16)
        grad_preact = (g_ref[...].astype(jnp.float32) * grown).astype(jnp.bfloat16)
        gp_ref[...] = grad_preact
        back = jnp.dot(grad_preact, wt_ref[...], preferred_element_type=jnp.float32)
        back_ref[...] = (back[:, :SIDE] * inv_root).astype(jnp.bfloat16)
        self_ref[...] = back[:, SIDE:]

    return kernel


def backward_kernel(wheres, block_rows):
    count = len(wheres)

    def kernel(cols_ref, count_ref, place_ref, vals_ref, self_ref, *rest):
        piece_refs = rest[:count]
        out_ref, slab, sems = rest[count:]
        t = pl.program_id(0)

        @pl.when(t == 0)
        def _():
            fill_slab(place_ref, piece_refs, wheres, slab, sems, block_rows)

        acc = row_product(t, cols_ref, count_ref, vals_ref, slab, False)
        out_ref[...] = (acc + self_ref[...]).astype(jnp.bfloat16)

    return kernel


def weight_kernel(scale):
    def kernel(both_ref, gp_ref, out_ref):
        gp = gp_ref[...]
        weights = lax.dot_general(
            both_ref[...], gp, (((0,), (0,)), ((), ())), preferred_element_type=jnp.float32
        )
        bias = jnp.sum(gp.astype(jnp.float32), axis=0, keepdims=True)
        rows = 2 * SIDE
        for p in range(8):
            out_ref[p, 0:32] = weights[p * 32 : (p + 1) * 32] * scale
            out_ref[p, 32:40] = jnp.broadcast_to(bias, (8, rows)) * scale

    return kernel


def whole(shape):
    return pl.BlockSpec(shape, lambda t, *_: (0,) * len(shape))


def by_row(shape):
    return pl.BlockSpec(shape, lambda t, *_: (t,) + (0,) * (len(shape) - 1))


def mesh_perm(dx, dy, dz, dk):
    def index(x, y, z, k):
        return ((x % 4) * 2 + (y % 2)) * 32 + (z % 8) * 4 + ((y // 2) % 2) * 2 + (k % 2)

    return [
        (index(x, y, z, k), index(x + dx, (y + dy) % 4, z + dz, k + dk))
        for x in range(4)
        for y in range(4)
        for z in range(8)
        for k in range(2)
    ]


def shift(a, dx, dy, dz, dk):
    return lax.ppermute(a, ("row", "col"), mesh_perm(dx, dy, dz, dk))


def rolled_sum(parts, place):
    n = len(parts)
    stacked = jnp.stack(parts[::-1] + parts[::-1])
    first = lax.rem(n - 1 - place + n, n)
    ordered = lax.dynamic_slice_in_dim(stacked, first, n, 0)
    total = ordered[0]
    for i in range(1, n):
        total = total + ordered[i]
    return total


def sum_everywhere(parts8, x, y, z, k):
    me = x * 2 + k

    def piece(dx, dk):
        p = lax.rem(x + dx, 4) * 2 + lax.rem(k + dk, 2)
        return lax.dynamic_index_in_dim(parts8, p, 0, keepdims=False)

    total = lax.dynamic_index_in_dim(parts8, me, 0, keepdims=False)
    for dx in range(4):
        for dk in range(2):
            if dx or dk:
                total = total + shift(piece(dx, dk), dx, 0, 0, dk)
    total = rolled_sum([total] + [shift(total, 0, d, 0, 0) for d in range(1, 4)], y)
    total = rolled_sum([total] + [shift(total, 0, 0, d, 0) for d in range(1, 8)], z)
    columns = []
    for dx in range(4):
        same = shift(total, dx, 0, 0, 0) if dx else total
        other = shift(total, dx, 0, 0, 1)
        columns.append(jnp.where(k == 0, jnp.stack([same, other]), jnp.stack([other, same])))
    stacked = jnp.stack(columns[::-1] + columns[::-1])
    ordered = lax.dynamic_slice_in_dim(stacked, lax.rem(3 - x + 4, 4), 4, 0)
    return ordered.reshape(parts8.shape)


def on_device(node_feat, tile_cols, tile_vals, tile_count, w_self, w_neigh, layer_bias, grad_out):
    rows, features = node_feat.shape
    hidden = grad_out.shape[1]
    tile_rows, slots = tile_cols.shape
    slab_rows = rows * lax.axis_size("col")
    grad_scale = 1.0 / math.sqrt(rows * lax.axis_size("row") * lax.axis_size("col"))
    r, c = lax.axis_index("row"), lax.axis_index("col")
    x, y_lo, z, y_hi, core = r // 2, r % 2, c // 4, (c // 2) % 2, c % 2
    place = jnp.stack([z, y_hi, core]).astype(jnp.int32)
    params = pltpu.CompilerParams(
        dimension_semantics=("arbitrary",), vmem_limit_bytes=40 * 1024 * 1024
    )
    vals_spec = by_row((1, slots, SIDE, SIDE))

    w_both = jnp.concatenate([w_self, w_neigh], axis=0)
    w_back = jnp.concatenate([w_neigh.T, w_self.T], axis=1)

    pieces = gather_slab(node_feat)
    wheres = [w for _, w in pieces]
    n_copies = sum(len(w) for w in wheres)
    any_spec = pl.BlockSpec(memory_space=pl.ANY)
    scratch = [
        pltpu.VMEM((slab_rows, features), jnp.bfloat16),
        pltpu.SemaphoreType.DMA((n_copies,)),
    ]
    activation, scaled_back, self_back, both, grad_preact = pl.pallas_call(
        forward_kernel(wheres, rows),
        grid_spec=pltpu.PrefetchScalarGridSpec(
            num_scalar_prefetch=3,
            grid=(tile_rows,),
            in_specs=[
                vals_spec,
                by_row((SIDE, features)),
                by_row((SIDE, hidden)),
                whole((2 * features, hidden)),
                whole((hidden, 2 * features)),
                whole((1, hidden)),
            ]
            + [any_spec] * len(pieces),
            out_specs=[
                by_row((SIDE, hidden)),
                by_row((SIDE, features)),
                by_row((SIDE, features)),
                by_row((SIDE, 2 * features)),
                by_row((SIDE, hidden)),
            ],
            scratch_shapes=scratch,
        ),
        out_shape=[
            jax.ShapeDtypeStruct((rows, hidden), jnp.bfloat16),
            jax.ShapeDtypeStruct((rows, features), jnp.bfloat16),
            jax.ShapeDtypeStruct((rows, features), jnp.float32),
            jax.ShapeDtypeStruct((rows, 2 * features), jnp.bfloat16),
            jax.ShapeDtypeStruct((rows, hidden), jnp.bfloat16),
        ],
        compiler_params=params,
        name="forward",
    )(
        tile_cols, tile_count, place, tile_vals, node_feat, grad_out, w_both, w_back,
        layer_bias.reshape(1, hidden), *[a for a, _ in pieces],
    )

    terms = pl.pallas_call(
        weight_kernel(grad_scale),
        out_shape=jax.ShapeDtypeStruct((8, 40, hidden), jnp.float32),
        compiler_params=pltpu.CompilerParams(vmem_limit_bytes=16 * 1024 * 1024),
        cost_estimate=pl.CostEstimate(
            flops=2 * rows * hidden * hidden, bytes_accessed=4 * rows * hidden, transcendentals=0
        ),
        name="weights",
    )(both, grad_preact)

    back_pieces = gather_slab(scaled_back)
    totals = sum_everywhere(terms, x, y_hi * 2 + y_lo, z, core)
    weights = totals[:, :32].reshape(2 * features, hidden)
    bias = totals[0, 32]

    grad_feat = pl.pallas_call(
        backward_kernel(wheres, rows),
        grid_spec=pltpu.PrefetchScalarGridSpec(
            num_scalar_prefetch=3,
            grid=(tile_rows,),
            in_specs=[vals_spec, by_row((SIDE, features))] + [any_spec] * len(pieces),
            out_specs=by_row((SIDE, features)),
            scratch_shapes=scratch,
        ),
        out_shape=jax.ShapeDtypeStruct((rows, features), jnp.bfloat16),
        compiler_params=params,
        name="backward",
    )(tile_cols, tile_count, place, tile_vals, self_back, *[a for a, _ in back_pieces])
    return activation, grad_feat, weights[:features], weights[features:], bias


def solution(mesh):
    return jax.shard_map(
        on_device,
        mesh=mesh,
        in_specs=(
            P(("row", "col"), None),
            P(("row", "col"), None),
            P(("row", "col"), None, None, None),
            P(("row", "col")),
            P(),
            P(),
            P(),
            P(("row", "col"), None),
        ),
        out_specs=(P(("row", "col"), None), P(("row", "col"), None), P(), P(), P()),
        check_vma=False,
    )
```

```python
import math

import jax
import jax.numpy as jnp
from jax import lax
from jax.experimental import pallas as pl
from jax.experimental.pallas import tpu as pltpu
from jax.sharding import PartitionSpec as P

SIDE = 128
GROUP = 8
ROW_CHUNK = 256


def col_index(z, y, k):
    return (z % 8) * 4 + (y % 2) * 2 + (k % 2)


def col_move(x, place_after):
    pairs = [
        (col_index(z, y, k), col_index(*place_after(z, y, k)))
        for z in range(8)
        for y in range(2)
        for k in range(2)
    ]
    return lax.ppermute(x, "col", pairs)


def swap_cores(x):
    return col_move(x, lambda z, y, k: (z, y, k + 1))


def swap_y(x):
    return col_move(x, lambda z, y, k: (z, y + 1, k))


def step_z(x):
    return col_move(x, lambda z, y, k: (z + 1 - 2 * k, y, k))


def after(x, *others):
    return lax.optimization_barrier((x,) + others)[0]


def gather_slab(x, ready):
    other = swap_cores(x)
    far = swap_y(after(x, other))
    chains = [(x, 0, 0), (other, 0, 1), (far, 1, 0), (swap_cores(far), 1, 1)]
    pieces = [(a, (0, y, k, 0)) for a, y, k in chains]
    chains[2] = (after(far, *ready), 1, 0)
    marks = [other]
    for steps in range(1, 5):
        if steps == 4:
            chains = [c for c in chains if c[2] == 0]
        chains = [(step_z(a), y, k) for a, y, k in chains]
        for a, y, k in chains:
            pieces.append((a, (steps, y, k, 0)))
            pieces.append((swap_cores(a), (steps, y, 1 - k, 1)))
            if k == 0:
                marks.append(a)
    return pieces, marks


def near(pieces):
    return [pltpu.with_memory_space_constraint(a, pltpu.HBM) for a, _ in pieces]


def slab_copies(place_ref, piece_refs, origins, slab, sems):
    z, y, k = place_ref[0], place_ref[1], place_ref[2]
    rows = slab.shape[0] // 32
    copies = []
    for i, (ref, (steps, y_flip, k_flip, crossed)) in enumerate(zip(piece_refs, origins)):
        way = 2 * lax.rem(k + crossed, 2) - 1
        home = lax.rem(z + way * steps + 8, 8) * 4 + lax.rem(y + y_flip, 2) * 2 + lax.rem(k + k_flip, 2)
        start = pl.multiple_of(home * rows, SIDE)
        copies.append(pltpu.make_async_copy(ref, slab.at[pl.ds(start, rows)], sems.at[i]))
    return copies


def fetch_groups(count_ref, vals_ref, buf, sems):
    def group_copy(t, i):
        part = pl.ds(i * GROUP, GROUP)
        return pltpu.make_async_copy(vals_ref.at[t, part], buf.at[t, part], sems.at[t, i])

    def trips(t):
        return (count_ref[t] + (GROUP - 1)) // GROUP

    def fetch(t, _):
        def one(i, _):
            group_copy(t, i).start()
            return 0

        return lax.fori_loop(0, trips(t), one, 0)

    lax.fori_loop(0, buf.shape[0], fetch, 0)
    return group_copy, trips


def products(cols_ref, count_ref, vals_ref, copies, slab, buf, sems, out):
    for c in copies:
        c.start()
    group_copy, trips = fetch_groups(count_ref, vals_ref, buf, sems)
    for c in copies:
        c.wait()

    def row(t, _):
        def group(i, acc):
            group_copy(t, i).wait()
            left, right = [], []
            for j in range(GROUP):
                slot = i * GROUP + j
                left.append(buf[t, slot])
                start = pl.multiple_of(cols_ref[t, slot] * SIDE, SIDE)
                right.append(slab[pl.ds(start, SIDE), :])
            lhs, rhs = jnp.concatenate(left, axis=1), jnp.concatenate(right, axis=0)
            return acc + jnp.dot(lhs, rhs, preferred_element_type=jnp.float32)

        acc = lax.fori_loop(0, trips(t), group, jnp.zeros((SIDE, SIDE), jnp.float32))
        out[pl.ds(pl.multiple_of(t * SIDE, SIDE), SIDE), :] = acc
        return 0

    lax.fori_loop(0, buf.shape[0], row, 0)


def forward_kernel(origins):
    count = len(origins)

    def kernel(cols_ref, count_ref, place_ref, vals_ref, x_ref, g_ref, inv_ref, w_ref, wt_ref, bias_ref, *rest):
        piece_refs = rest[:count]
        act_ref, back_ref, self_ref, both_ref, gp_ref, slab, buf, total, slab_sems, sems = rest[count:]
        copies = slab_copies(place_ref, piece_refs, origins, slab, slab_sems)
        products(cols_ref, count_ref, vals_ref, copies, slab, buf, sems, total)
        for chunk in range(x_ref.shape[0] // ROW_CHUNK):
            part = pl.ds(chunk * ROW_CHUNK, ROW_CHUNK)
            inv_root = inv_ref[part, :]
            aggregated = (total[part, :] * inv_root).astype(jnp.bfloat16)
            both = jnp.concatenate([x_ref[part, :], aggregated], axis=1)
            both_ref[part, :] = both
            preact = jnp.dot(both, w_ref[...], preferred_element_type=jnp.float32) + bias_ref[...]
            grown = jnp.exp(jnp.minimum(preact, 0.0))
            act_ref[part, :] = jnp.where(preact > 0.0, preact, grown - 1.0).astype(jnp.bfloat16)
            grad_preact = (g_ref[part, :].astype(jnp.float32) * grown).astype(jnp.bfloat16)
            gp_ref[part, :] = grad_preact
            back = jnp.dot(grad_preact, wt_ref[...], preferred_element_type=jnp.float32)
            back_ref[part, :] = (back[:, :SIDE] * inv_root).astype(jnp.bfloat16)
            self_ref[part, :] = back[:, SIDE:]

    return kernel


def backward_kernel(origins):
    count = len(origins)

    def kernel(cols_ref, count_ref, place_ref, vals_ref, self_ref, *rest):
        piece_refs = rest[:count]
        out_ref, slab, buf, total, slab_sems, sems = rest[count:]
        copies = slab_copies(place_ref, piece_refs, origins, slab, slab_sems)
        products(cols_ref, count_ref, vals_ref, copies, slab, buf, sems, total)
        out_ref[...] = (total[...] + self_ref[...]).astype(jnp.bfloat16)

    return kernel


def degree_kernel(count_ref, vals_ref, out_ref, buf, sems):
    ones = jnp.ones((GROUP * SIDE, SIDE), jnp.bfloat16)
    group_copy, trips = fetch_groups(count_ref, vals_ref, buf, sems)

    def row(t, _):
        def group(i, acc):
            group_copy(t, i).wait()
            lhs = jnp.concatenate([buf[t, i * GROUP + j] for j in range(GROUP)], axis=1)
            return acc + jnp.dot(lhs, ones, preferred_element_type=jnp.float32)

        degree = lax.fori_loop(0, trips(t), group, jnp.zeros((SIDE, SIDE), jnp.float32))
        out_ref[pl.ds(pl.multiple_of(t * SIDE, SIDE), SIDE), :] = lax.rsqrt(degree)
        return 0

    lax.fori_loop(0, buf.shape[0], row, 0)


def weight_kernel(scale):
    def kernel(both_ref, gp_ref, out_ref):
        gp = gp_ref[...]
        weights = lax.dot_general(
            both_ref[...], gp, (((0,), (0,)), ((), ())), preferred_element_type=jnp.float32
        )
        bias = jnp.sum(gp.astype(jnp.float32), axis=0, keepdims=True)
        for p in range(8):
            out_ref[p // 4, p % 4, 0:32] = weights[p * 32 : (p + 1) * 32] * scale
            out_ref[p // 4, p % 4, 32:40] = jnp.broadcast_to(bias, (8, bias.shape[1])) * scale

    return kernel


def mesh_move(a, place_after):
    def index(x, y, z, k):
        return ((x % 4) * 2 + (y % 2)) * 32 + (z % 8) * 4 + ((y // 2) % 2) * 2 + (k % 2)

    pairs = [
        (index(x, y, z, k), index(*place_after(x, y, z, k)))
        for x in range(4)
        for y in range(4)
        for z in range(8)
        for k in range(2)
    ]
    return lax.ppermute(a, ("row", "col"), pairs)


def move_x(a, dx):
    return mesh_move(a, lambda x, y, z, k: (x + dx, y, z, k))


def join_kernel(x_ref, *refs):
    out_ref = refs[-1]
    for dx in range(4):
        out_ref[lax.rem(x_ref[0] + 4 - dx, 4)] = refs[dx][...]


def sum_everywhere(terms, x, k, marks):
    def own(a, i):
        return lax.dynamic_index_in_dim(a, i, 0, keepdims=False)

    def flip(a, y_bit, z_bit):
        return a + mesh_move(a, lambda x, y, z, k: (x, y ^ y_bit, z ^ z_bit, k))

    terms = after(terms, marks[0])
    half = own(terms, k) + mesh_move(own(terms, 1 - k), lambda x, y, z, k: (x, y, z, 1 - k))
    half = after(half, marks[1])
    part = own(half, x)
    for dx in range(1, 4):
        part = part + move_x(own(half, lax.rem(x + dx, 4)), dx)
    for mark, (y_bit, z_bit) in zip(marks[2:7], ((1, 0), (2, 0), (0, 1), (0, 2), (0, 4))):
        part = flip(after(part, mark), y_bit, z_bit)
    part = after(part, marks[7])
    half = pl.pallas_call(
        join_kernel,
        in_specs=[pl.BlockSpec(memory_space=pltpu.SMEM)] + [pl.BlockSpec(memory_space=pltpu.VMEM)] * 4,
        out_specs=pl.BlockSpec(memory_space=pltpu.VMEM),
        out_shape=jax.ShapeDtypeStruct(terms.shape[1:], jnp.float32),
        name="join",
    )(x.reshape(1), part, *[move_x(part, dx) for dx in range(1, 4)])
    got = mesh_move(half, lambda x, y, z, k: (x, y, z, 1 - k))
    return jnp.where(k == 0, half, got), jnp.where(k == 0, got, half)


def on_device(node_feat, tile_cols, tile_vals, tile_count, w_self, w_neigh, layer_bias, grad_out):
    rows, features = node_feat.shape
    hidden = grad_out.shape[1]
    tile_rows, slots = tile_cols.shape
    slab_rows = rows * lax.axis_size("col")
    grad_scale = 1.0 / math.sqrt(rows * lax.axis_size("row") * lax.axis_size("col"))
    r, c = lax.axis_index("row"), lax.axis_index("col")
    x, z, y_hi, core = r // 2, c // 4, (c // 2) % 2, c % 2
    place = jnp.stack([z, y_hi, core]).astype(jnp.int32)
    params = pltpu.CompilerParams(vmem_limit_bytes=32 * 1024 * 1024)

    w_both = jnp.concatenate([w_self, w_neigh], axis=0)
    w_back = jnp.concatenate([w_neigh.T, w_self.T], axis=1)

    smem = pl.BlockSpec(memory_space=pltpu.SMEM)
    vmem = pl.BlockSpec(memory_space=pltpu.VMEM)
    hbm = pl.BlockSpec(memory_space=pltpu.HBM)
    any_space = pl.BlockSpec(memory_space=pl.ANY)
    tile_vals = pltpu.with_memory_space_constraint(tile_vals, pltpu.HBM)
    vals_scratch = [
        pltpu.VMEM((tile_rows, slots, SIDE, SIDE), jnp.bfloat16),
        pltpu.SemaphoreType.DMA((tile_rows, slots // GROUP)),
    ]
    inv_root = pl.pallas_call(
        degree_kernel,
        in_specs=[smem, hbm],
        out_specs=vmem,
        scratch_shapes=vals_scratch,
        out_shape=jax.ShapeDtypeStruct((rows, SIDE), jnp.float32),
        compiler_params=pltpu.CompilerParams(vmem_limit_bytes=20 * 1024 * 1024),
        name="degree",
    )(tile_count, tile_vals)

    pieces, _ = gather_slab(node_feat, [inv_root])
    origins = [o for _, o in pieces]
    scratch = [
        pltpu.VMEM((slab_rows, features), jnp.bfloat16),
        vals_scratch[0],
        pltpu.VMEM((rows, features), jnp.float32),
        pltpu.SemaphoreType.DMA((len(pieces),)),
        vals_scratch[1],
    ]
    activation, scaled_back, self_back, both, grad_preact = pl.pallas_call(
        forward_kernel(origins),
        in_specs=[smem] * 3 + [hbm] + [vmem] * 6 + [any_space] * len(pieces),
        out_specs=[vmem] * 5,
        scratch_shapes=scratch,
        out_shape=[
            jax.ShapeDtypeStruct((rows, hidden), jnp.bfloat16),
            jax.ShapeDtypeStruct((rows, features), jnp.bfloat16),
            jax.ShapeDtypeStruct((rows, features), jnp.float32),
            jax.ShapeDtypeStruct((rows, 2 * features), jnp.bfloat16),
            jax.ShapeDtypeStruct((rows, hidden), jnp.bfloat16),
        ],
        compiler_params=params,
        name="forward",
    )(
        tile_cols, tile_count, place, tile_vals, node_feat, grad_out, inv_root, w_both, w_back,
        layer_bias.reshape(1, hidden), *near(pieces),
    )

    back_pieces, marks = gather_slab(scaled_back, [])
    terms = pl.pallas_call(
        weight_kernel(grad_scale),
        out_shape=jax.ShapeDtypeStruct((2, 4, 40, hidden), jnp.float32),
        compiler_params=pltpu.CompilerParams(vmem_limit_bytes=8 * 1024 * 1024),
        name="weights",
    )(both, grad_preact)
    self_total, neigh_total = sum_everywhere(terms, x, core, marks)

    grad_feat = pl.pallas_call(
        backward_kernel(origins),
        in_specs=[smem] * 3 + [hbm, vmem] + [any_space] * len(pieces),
        out_specs=vmem,
        scratch_shapes=scratch,
        out_shape=jax.ShapeDtypeStruct((rows, features), jnp.bfloat16),
        compiler_params=params,
        name="backward",
    )(tile_cols, tile_count, place, tile_vals, self_back, *near(back_pieces))
    return (
        activation,
        grad_feat,
        self_total[:, :32].reshape(features, hidden),
        neigh_total[:, :32].reshape(features, hidden),
        self_total[0, 32],
    )


def solution(mesh):
    return jax.shard_map(
        on_device,
        mesh=mesh,
        in_specs=(
            P(("row", "col"), None),
            P(("row", "col"), None),
            P(("row", "col"), None, None, None),
            P(("row", "col")),
            P(),
            P(),
            P(),
            P(("row", "col"), None),
        ),
        out_specs=(P(("row", "col"), None), P(("row", "col"), None), P(), P(), P()),
        check_vma=False,
    )
```

```python
import math

import jax
import jax.numpy as jnp
from jax import lax
from jax.experimental import pallas as pl
from jax.experimental.pallas import tpu as pltpu
from jax.sharding import PartitionSpec as P

SIDE = 128
GROUP = 10
MARKS = (0, 1, 3, 5, 7, 9, 11, 13)
ROW_CHUNK = 256


def col_index(z, y, k):
    return (z % 8) * 4 + (y % 2) * 2 + (k % 2)


def col_move(x, place_after):
    pairs = [
        (col_index(z, y, k), col_index(*place_after(z, y, k)))
        for z in range(8)
        for y in range(2)
        for k in range(2)
    ]
    return lax.ppermute(x, "col", pairs)


def swap_cores(x):
    return col_move(x, lambda z, y, k: (z, y, k + 1))


def swap_y(x):
    return col_move(x, lambda z, y, k: (z, y + 1, k))


def step_z(x):
    return col_move(x, lambda z, y, k: (z + 1 - 2 * k, y, k))


def after(x, *others):
    return lax.optimization_barrier((x,) + others)[0]


def gather_slab(x, ready):
    other = swap_cores(x)
    far = swap_y(after(x, other))
    chains = [(x, 0, 0), (other, 0, 1), (far, 1, 0), (swap_cores(far), 1, 1)]
    pieces = [(a, (0, y, k, 0)) for a, y, k in chains]
    chains[2] = (after(far, *ready), 1, 0)
    marks = [other]
    for steps in range(1, 5):
        if steps == 4:
            chains = [c for c in chains if c[2] == 0]
        chains = [(step_z(a), y, k) for a, y, k in chains]
        for a, y, k in chains:
            pieces.append((a, (steps, y, k, 0)))
            pieces.append((swap_cores(a), (steps, y, 1 - k, 1)))
            marks.append(a)
    return pieces, marks


def near(pieces):
    return [pltpu.with_memory_space_constraint(a, pltpu.HBM) for a, _ in pieces]


def slab_copies(place_ref, piece_refs, origins, slab, sems):
    z, y, k = place_ref[0], place_ref[1], place_ref[2]
    rows = slab.shape[0] // 32
    copies = []
    for i, (ref, (steps, y_flip, k_flip, crossed)) in enumerate(zip(piece_refs, origins)):
        way = 2 * lax.rem(k + crossed, 2) - 1
        home = lax.rem(z + way * steps + 8, 8) * 4 + lax.rem(y + y_flip, 2) * 2 + lax.rem(k + k_flip, 2)
        start = pl.multiple_of(home * rows, SIDE)
        copies.append(pltpu.make_async_copy(ref, slab.at[pl.ds(start, rows)], sems.at[i]))
    return copies


def fetch_groups(count_ref, vals_ref, buf, sems):
    def group_copy(t, i):
        part = pl.ds(i * GROUP, GROUP)
        return pltpu.make_async_copy(vals_ref.at[t, part], buf.at[t, part], sems.at[t, i])

    def trips(t):
        return (count_ref[t] + (GROUP - 1)) // GROUP

    def fetch(t, _):
        def one(i, _):
            group_copy(t, i).start()
            return 0

        return lax.fori_loop(0, trips(t), one, 0)

    lax.fori_loop(0, buf.shape[0], fetch, 0)
    return group_copy, trips


def products(cols_ref, count_ref, vals_ref, copies, slab, buf, sems, out):
    for c in copies:
        c.start()
    group_copy, trips = fetch_groups(count_ref, vals_ref, buf, sems)
    for c in copies:
        c.wait()

    def row(t, _):
        def group(i, acc):
            group_copy(t, i).wait()
            left, right = [], []
            for j in range(GROUP):
                slot = i * GROUP + j
                left.append(buf[t, slot])
                start = pl.multiple_of(cols_ref[t, slot] * SIDE, SIDE)
                right.append(slab[pl.ds(start, SIDE), :])
            lhs, rhs = jnp.concatenate(left, axis=1), jnp.concatenate(right, axis=0)
            return acc + jnp.dot(lhs, rhs, preferred_element_type=jnp.float32)

        acc = lax.fori_loop(0, trips(t), group, jnp.zeros((SIDE, SIDE), jnp.float32))
        out[pl.ds(pl.multiple_of(t * SIDE, SIDE), SIDE), :] = acc
        return 0

    lax.fori_loop(0, buf.shape[0], row, 0)


def forward_kernel(origins):
    count = len(origins)

    def kernel(cols_ref, count_ref, place_ref, vals_ref, x_ref, g_ref, inv_ref, w_ref, wt_ref, bias_ref, *rest):
        piece_refs = rest[:count]
        act_ref, back_ref, self_ref, both_ref, gp_ref, slab, buf, total, slab_sems, sems = rest[count:]
        copies = slab_copies(place_ref, piece_refs, origins, slab, slab_sems)
        products(cols_ref, count_ref, vals_ref, copies, slab, buf, sems, total)
        for chunk in range(x_ref.shape[0] // ROW_CHUNK):
            part = pl.ds(chunk * ROW_CHUNK, ROW_CHUNK)
            inv_root = inv_ref[part, :]
            aggregated = (total[part, :] * inv_root).astype(jnp.bfloat16)
            both = jnp.concatenate([x_ref[part, :], aggregated], axis=1)
            both_ref[part, :] = both
            preact = jnp.dot(both, w_ref[...], preferred_element_type=jnp.float32) + bias_ref[...]
            grown = jnp.exp(jnp.minimum(preact, 0.0))
            act_ref[part, :] = jnp.where(preact > 0.0, preact, grown - 1.0).astype(jnp.bfloat16)
            grad_preact = (g_ref[part, :].astype(jnp.float32) * grown).astype(jnp.bfloat16)
            gp_ref[part, :] = grad_preact
            back = jnp.dot(grad_preact, wt_ref[...], preferred_element_type=jnp.float32)
            back_ref[part, :] = (back[:, :SIDE] * inv_root).astype(jnp.bfloat16)
            self_ref[part, :] = back[:, SIDE:]

    return kernel


def backward_kernel(origins):
    count = len(origins)

    def kernel(cols_ref, count_ref, place_ref, vals_ref, self_ref, *rest):
        piece_refs = rest[:count]
        out_ref, slab, buf, total, slab_sems, sems = rest[count:]
        copies = slab_copies(place_ref, piece_refs, origins, slab, slab_sems)
        products(cols_ref, count_ref, vals_ref, copies, slab, buf, sems, total)
        out_ref[...] = (total[...] + self_ref[...]).astype(jnp.bfloat16)

    return kernel


def degree_kernel(count_ref, vals_ref, out_ref, buf, sems):
    ones = jnp.ones((GROUP * SIDE, SIDE), jnp.bfloat16)
    group_copy, trips = fetch_groups(count_ref, vals_ref, buf, sems)

    def row(t, _):
        def group(i, acc):
            group_copy(t, i).wait()
            lhs = jnp.concatenate([buf[t, i * GROUP + j] for j in range(GROUP)], axis=1)
            return acc + jnp.dot(lhs, ones, preferred_element_type=jnp.float32)

        degree = lax.fori_loop(0, trips(t), group, jnp.zeros((SIDE, SIDE), jnp.float32))
        out_ref[pl.ds(pl.multiple_of(t * SIDE, SIDE), SIDE), :] = lax.rsqrt(degree)
        return 0

    lax.fori_loop(0, buf.shape[0], row, 0)


def weight_kernel(scale):
    def kernel(both_ref, gp_ref, out_ref):
        gp = gp_ref[...]
        weights = lax.dot_general(
            both_ref[...], gp, (((0,), (0,)), ((), ())), preferred_element_type=jnp.float32
        )
        bias = jnp.sum(gp.astype(jnp.float32), axis=0, keepdims=True)
        for p in range(8):
            out_ref[p // 4, p % 4, 0:32] = weights[p * 32 : (p + 1) * 32] * scale
            out_ref[p // 4, p % 4, 32:40] = jnp.broadcast_to(bias, (8, bias.shape[1])) * scale

    return kernel


def mesh_move(a, place_after):
    def index(x, y, z, k):
        return ((x % 4) * 2 + (y % 2)) * 32 + (z % 8) * 4 + ((y // 2) % 2) * 2 + (k % 2)

    pairs = [
        (index(x, y, z, k), index(*place_after(x, y, z, k)))
        for x in range(4)
        for y in range(4)
        for z in range(8)
        for k in range(2)
    ]
    return lax.ppermute(a, ("row", "col"), pairs)


def move_x(a, dx):
    return mesh_move(a, lambda x, y, z, k: (x + dx, y, z, k))


def join_kernel(x_ref, *refs):
    out_ref = refs[-1]
    for dx in range(4):
        out_ref[lax.rem(x_ref[0] + 4 - dx, 4)] = refs[dx][...]


def finish_kernel(k_ref, half_ref, got_ref, self_ref, neigh_ref, bias_ref):
    own_first = k_ref[0] == 0
    rows = self_ref.shape[0] // 4
    for p in range(4):
        half, got = half_ref[p], got_ref[p]
        self_ref[p * rows : (p + 1) * rows] = jnp.where(own_first, half, got)[:rows]
        neigh_ref[p * rows : (p + 1) * rows] = jnp.where(own_first, got, half)[:rows]
    bias_ref[...] = jnp.where(own_first, half_ref[0], got_ref[0])[rows : rows + 1]


def sum_everywhere(terms, x, k, marks):
    def own(a, i):
        return lax.dynamic_index_in_dim(a, i, 0, keepdims=False)

    def flip(a, y_bit, z_bit):
        return a + mesh_move(a, lambda x, y, z, k: (x, y ^ y_bit, z ^ z_bit, k))

    terms = after(terms, marks[MARKS[0]])
    half = own(terms, k) + mesh_move(own(terms, 1 - k), lambda x, y, z, k: (x, y, z, 1 - k))
    half = after(half, marks[MARKS[1]])
    part = own(half, x)
    for dx in range(1, 4):
        part = part + move_x(own(half, lax.rem(x + dx, 4)), dx)
    for mark, (y_bit, z_bit) in zip([marks[m] for m in MARKS[2:7]], ((1, 0), (2, 0), (0, 1), (0, 2), (0, 4))):
        part = flip(after(part, mark), y_bit, z_bit)
    part = after(part, marks[MARKS[7]])
    half = pl.pallas_call(
        join_kernel,
        in_specs=[pl.BlockSpec(memory_space=pltpu.SMEM)] + [pl.BlockSpec(memory_space=pltpu.VMEM)] * 4,
        out_specs=pl.BlockSpec(memory_space=pltpu.VMEM),
        out_shape=jax.ShapeDtypeStruct(terms.shape[1:], jnp.float32),
        name="join",
    )(x.reshape(1), part, *[move_x(part, dx) for dx in range(1, 4)])
    got = mesh_move(half, lambda x, y, z, k: (x, y, z, 1 - k))
    rows, lanes = terms.shape[2] - 8, terms.shape[3]
    return pl.pallas_call(
        finish_kernel,
        in_specs=[pl.BlockSpec(memory_space=pltpu.SMEM)] + [pl.BlockSpec(memory_space=pltpu.VMEM)] * 2,
        out_specs=[pl.BlockSpec(memory_space=pltpu.VMEM)] * 3,
        out_shape=[
            jax.ShapeDtypeStruct((4 * rows, lanes), jnp.float32),
            jax.ShapeDtypeStruct((4 * rows, lanes), jnp.float32),
            jax.ShapeDtypeStruct((1, lanes), jnp.float32),
        ],
        name="finish",
    )(k.reshape(1), half, got)


def on_device(node_feat, tile_cols, tile_vals, tile_count, w_self, w_neigh, layer_bias, grad_out):
    rows, features = node_feat.shape
    hidden = grad_out.shape[1]
    tile_rows, slots = tile_cols.shape
    slab_rows = rows * lax.axis_size("col")
    grad_scale = 1.0 / math.sqrt(rows * lax.axis_size("row") * lax.axis_size("col"))
    r, c = lax.axis_index("row"), lax.axis_index("col")
    x, z, y_hi, core = r // 2, c // 4, (c // 2) % 2, c % 2
    place = jnp.stack([z, y_hi, core]).astype(jnp.int32)
    params = pltpu.CompilerParams(vmem_limit_bytes=32 * 1024 * 1024)

    w_both = jnp.concatenate([w_self, w_neigh], axis=0)
    w_back = jnp.concatenate([w_neigh.T, w_self.T], axis=1)

    smem = pl.BlockSpec(memory_space=pltpu.SMEM)
    vmem = pl.BlockSpec(memory_space=pltpu.VMEM)
    hbm = pl.BlockSpec(memory_space=pltpu.HBM)
    any_space = pl.BlockSpec(memory_space=pl.ANY)
    tile_vals = pltpu.with_memory_space_constraint(tile_vals, pltpu.HBM)
    vals_scratch = [
        pltpu.VMEM((tile_rows, slots, SIDE, SIDE), jnp.bfloat16),
        pltpu.SemaphoreType.DMA((tile_rows, slots // GROUP)),
    ]
    inv_root = pl.pallas_call(
        degree_kernel,
        in_specs=[smem, hbm],
        out_specs=vmem,
        scratch_shapes=vals_scratch,
        out_shape=jax.ShapeDtypeStruct((rows, SIDE), jnp.float32),
        compiler_params=pltpu.CompilerParams(vmem_limit_bytes=20 * 1024 * 1024),
        name="degree",
    )(tile_count, tile_vals)

    pieces, _ = gather_slab(node_feat, [inv_root])
    origins = [o for _, o in pieces]
    scratch = [
        pltpu.VMEM((slab_rows, features), jnp.bfloat16),
        vals_scratch[0],
        pltpu.VMEM((rows, features), jnp.float32),
        pltpu.SemaphoreType.DMA((len(pieces),)),
        vals_scratch[1],
    ]
    activation, scaled_back, self_back, both, grad_preact = pl.pallas_call(
        forward_kernel(origins),
        in_specs=[smem] * 3 + [hbm] + [vmem] * 6 + [any_space] * len(pieces),
        out_specs=[vmem] * 5,
        scratch_shapes=scratch,
        out_shape=[
            jax.ShapeDtypeStruct((rows, hidden), jnp.bfloat16),
            jax.ShapeDtypeStruct((rows, features), jnp.bfloat16),
            jax.ShapeDtypeStruct((rows, features), jnp.float32),
            jax.ShapeDtypeStruct((rows, 2 * features), jnp.bfloat16),
            jax.ShapeDtypeStruct((rows, hidden), jnp.bfloat16),
        ],
        compiler_params=params,
        name="forward",
    )(
        tile_cols, tile_count, place, tile_vals, node_feat, grad_out, inv_root, w_both, w_back,
        layer_bias.reshape(1, hidden), *near(pieces),
    )

    back_pieces, marks = gather_slab(scaled_back, [])
    terms = pl.pallas_call(
        weight_kernel(grad_scale),
        out_shape=jax.ShapeDtypeStruct((2, 4, 40, hidden), jnp.float32),
        compiler_params=pltpu.CompilerParams(vmem_limit_bytes=8 * 1024 * 1024),
        name="weights",
    )(both, grad_preact)
    self_total, neigh_total, bias_total = sum_everywhere(terms, x, core, marks)

    grad_feat = pl.pallas_call(
        backward_kernel(origins),
        in_specs=[smem] * 3 + [hbm, vmem] + [any_space] * len(pieces),
        out_specs=vmem,
        scratch_shapes=scratch,
        out_shape=jax.ShapeDtypeStruct((rows, features), jnp.bfloat16),
        compiler_params=params,
        name="backward",
    )(tile_cols, tile_count, place, tile_vals, self_back, *near(back_pieces))
    return activation, grad_feat, self_total, neigh_total, bias_total.reshape(hidden)


def solution(mesh):
    return jax.shard_map(
        on_device,
        mesh=mesh,
        in_specs=(
            P(("row", "col"), None),
            P(("row", "col"), None),
            P(("row", "col"), None, None, None),
            P(("row", "col")),
            P(),
            P(),
            P(),
            P(("row", "col"), None),
        ),
        out_specs=(P(("row", "col"), None), P(("row", "col"), None), P(), P(), P()),
        check_vma=False,
    )
```
